32 devices in a mesh: section: 2 (over core), dp: 4 (over y, x), seq: 4 (over z).
Axes of the slice: x: 2, y: 2, z: 4, core: 2. Of those that a mesh axis runs over, the one named last changes fastest.
Arguments:
- section_ends: bfloat16 [2, 2, 4, 1024, 512], P('section', None, 'dp', 'seq'), may hold values from -6 to 6
- live: int32 [2, 4], P(None, 'dp'), may hold values from 0 to 1, as said below
- norm_gains: bfloat16 [2, 2, 512], P('section', None, 'dp'), may hold values from 0.5 to 1.5
- offsets: bfloat16 [2, 6, 512], P('section', None, 'dp'), may hold values from -2.5 to 2.5
- expand_bias: bfloat16 [2, 2048], P('section', 'dp'), may hold values from -2.5 to 2.5
- query_key_value: bfloat16 [2, 512, 1536], P('section', 'dp'), may hold values from -0.25 to 0.25
- attention_out: bfloat16 [2, 512, 512], P('section', 'dp'), may hold values from -2 to 2
- expand_weight: bfloat16 [2, 512, 2048], P('section', 'dp'), may hold values from -0.25 to 0.25
- contract_weight: bfloat16 [2, 2048, 512], P('section', 'dp'), may hold values from -0.125 to 0.125
Outputs:
- section_edges: float32 [2, 2, 4, 1024, 512], P('section', None, 'dp', 'seq')
- grad_norm_gains: float32 [2, 2, 512], P('section', None, 'dp')
- grad_offsets: float32 [2, 6, 512], P('section', None, 'dp')
- grad_expand_bias: float32 [2, 2048], P('section', 'dp')
- grad_query_key_value: float32 [2, 512, 1536], P('section', 'dp')
- grad_attention_out: float32 [2, 512, 512], P('section', 'dp')
- grad_expand: float32 [2, 512, 2048], P('section', 'dp')
- grad_contract: float32 [2, 2048, 512], P('section', 'dp')
The draws below stay inside these ranges and needn't reach their ends.
Inputs may be any that keep to these rules, and one draw needn't show every extreme that they name: `live`: 0 marks an empty slot of a micro-batch; in every draw some slot is 0 and some is 1.
All inputs are finite; a program needn't handle non-finite values.
Results may differ from the reference program's by a relative error of at most 0.018.
Values may be sent and summed in bfloat16 or wider, within the bound.
A program may use at most 128 MiB of HBM per device.

```python
import jax
import jax.numpy as jnp
from jax import lax

D = 512
HEADS = 8
HD = 64
FF = 2048
MB = 2
SLOTS = 4
LENGTH = 1024


def draw_live(key, part):
    key = jax.random.fold_in(key, 11)
    key_base, key_first, key_second = jax.random.split(key, 3)
    total_slots = MB * SLOTS
    base = (jax.random.randint(key_base, (total_slots,), 0, 10) < 7).astype(jnp.int32)
    first_slot = jax.random.randint(key_first, (), 0, total_slots)
    second_slot = (first_slot + 1 + jax.random.randint(key_second, (), 0, total_slots - 1)) % total_slots
    places = jnp.arange(total_slots)
    base = jnp.where(places == first_slot, 1, base)
    base = jnp.where(places == second_slot, 0, base)
    return base.reshape(MB, SLOTS).astype(jnp.int32)


def shard_levels(own_key, shape, pieces, least, largest):
    level, own = 1.0, jax.random.fold_in(own_key, 6)
    for axis_at, blocks in pieces:
        steps = jnp.exp(jax.random.uniform(jax.random.fold_in(own, axis_at), (blocks,), jnp.float32, least / len(pieces), largest / len(pieces)))
        level = level * jnp.repeat(steps, shape[axis_at] // blocks).reshape([-1 if axis == axis_at else 1 for axis in range(len(shape))])
    return level


def bell_draw(key, dims, scale, most, shards=(), dtype=jnp.bfloat16):
    values = scale * jax.random.normal(key, dims, jnp.float32)
    if shards:
        values = values * shard_levels(key, dims, shards, -0.22, 0.18)
    return jnp.clip(values, -most, most).astype(dtype)


def setup_inputs(seed: int = 0) -> dict:
    arg_keys = jax.random.split(jax.random.key(seed), 10)
    return {
        "section_ends": bell_draw(arg_keys[0], (2, MB, SLOTS, LENGTH, D), 1.0, 6.0, ((0, 2), (2, 4), (3, 4))),
        "live": draw_live(jax.random.fold_in(arg_keys[9], 71), 0),
        "norm_gains": jnp.clip(1.0 + 0.1 * jax.random.normal(arg_keys[2], (2, 2, D), jnp.float32), 0.5, 1.5).astype(jnp.bfloat16),
        "offsets": bell_draw(arg_keys[3], (2, 6, D), 0.3, 2.5, ((0, 2), (2, 4))),
        "expand_bias": bell_draw(arg_keys[4], (2, FF), 0.3, 2.5, ((0, 2), (1, 4))),
        "query_key_value": bell_draw(arg_keys[5], (2, D, 3 * D), D ** -0.5, 0.25, ((0, 2), (1, 4))),
        "attention_out": bell_draw(arg_keys[6], (2, D, D), (D // 64) ** -0.5, 2.0, ((0, 2), (1, 4))),
        "expand_weight": bell_draw(arg_keys[7], (2, D, FF), D ** -0.5, 0.25, ((0, 2), (1, 4))),
        "contract_weight": bell_draw(arg_keys[8], (2, FF, D), FF ** -0.5, 0.125, ((0, 2), (1, 4))),
    }


EPSILON = 1e-05
PRECISE = lax.Precision.HIGHEST

@jax.custom_vjp
def low(v):
    return lax.optimization_barrier(v.astype(jnp.bfloat16)).astype(jnp.float32)

@jax.custom_vjp
def low_back(v):
    return v

def low_keep(v):
    return (low(v), None)

def low_pass(kept, grad):
    return (grad,)

def back_keep(v):
    return (v, None)

def back_low(kept, grad):
    return (low(grad),)
low.defvjp(low_keep, low_pass)
low_back.defvjp(back_keep, back_low)

def crossing(values):
    return low(low_back(values))

def layer_norm(values, gain, shift):
    row_mean = lax.optimization_barrier(jnp.mean(values, axis=-1, keepdims=True))
    centred = values - row_mean
    variance = lax.optimization_barrier(jnp.mean(centred * centred, axis=-1, keepdims=True))
    return centred * lax.rsqrt(variance + EPSILON) * gain + shift

def attention(packed):
    length = packed.shape[0]
    unpacked = packed.reshape(length, 3, HEADS, HD)
    queries = unpacked[:, 0]
    keys_all = unpacked[:, 1]
    values_all = unpacked[:, 2]
    scores = jnp.einsum('qhd,khd->hqk', queries, keys_all, precision=PRECISE) * HD ** (-0.5)
    scores = low_back(scores)
    position = jnp.arange(length)
    causal = position[None, :] <= position[:, None]
    scores = jnp.where(causal[None], scores, -1e+30)
    probabilities = low(jax.nn.softmax(scores, axis=-1))
    result = jnp.einsum('hqk,khd->qhd', probabilities, values_all, precision=PRECISE)
    return result.reshape(length, HEADS * HD)

def block_layer(params, tokens_in):
    gain_rows, shift_rows, bias_row, qkv_matrix, out_matrix, up_matrix, down_matrix = params
    normed = low(layer_norm(tokens_in, gain_rows[0], shift_rows[0]))
    qkv_bias = jnp.concatenate([shift_rows[1], jnp.zeros_like(shift_rows[1]), shift_rows[2]])
    packed = crossing(jnp.dot(normed, qkv_matrix, precision=PRECISE) + qkv_bias)
    attended = crossing(attention(packed))
    branch = low_back(jnp.dot(attended, out_matrix, precision=PRECISE) + shift_rows[3])
    hidden = tokens_in + branch
    normed_two = low(layer_norm(hidden, gain_rows[1], shift_rows[4]))
    upward = low_back(jnp.dot(normed_two, up_matrix, precision=PRECISE) + bias_row)
    activated = low(jax.nn.gelu(upward, approximate=True))
    branch_two = low_back(jnp.dot(activated, down_matrix, precision=PRECISE) + shift_rows[5])
    return hidden + branch_two

def two_sections(params, tokens_in):
    first = block_layer(jax.tree.map(lambda a: a[0], params), tokens_in)
    return block_layer(jax.tree.map(lambda a: a[1], params), crossing(first))

def reference(section_ends, live, norm_gains, offsets, expand_bias, query_key_value, attention_out, expand_weight, contract_weight):
    params = tuple((a.astype(jnp.float32) for a in (norm_gains, offsets, expand_bias, query_key_value, attention_out, expand_weight, contract_weight)))
    length = section_ends.shape[3]
    model_width = section_ends.shape[4]
    inputs_all = section_ends[0].astype(jnp.float32).reshape(-1, length, model_width)
    mask_all = live.astype(jnp.float32).reshape(-1, 1, 1)
    cotangent = section_ends[1].astype(jnp.float32).reshape(-1, length, model_width) * mask_all

    def whole(params_in, inputs_in):
        one_sequence = jax.checkpoint(lambda sequence: two_sections(params_in, sequence))
        return lax.map(one_sequence, inputs_in)
    outputs_all, pullback = jax.vjp(whole, params, inputs_all)
    grads, grad_inputs = pullback(cotangent)
    section_edges = jnp.stack([grad_inputs, outputs_all * mask_all]).reshape(section_ends.shape)
    return (section_edges, grads[0], grads[1], grads[2], grads[3], grads[4], grads[5], grads[6])
```

```python
import jax
import jax.numpy as jnp
from jax import lax
from jax.sharding import PartitionSpec as P

HD = 64


EPSILON = 1e-05


def layer_norm(values, gain, shift):
    row_mean = jnp.mean(values, axis=-1, keepdims=True)
    centred = values - row_mean
    variance = jnp.mean(centred * centred, axis=-1, keepdims=True)
    inverse = lax.rsqrt(variance + EPSILON)
    normal = centred * inverse
    return (normal * gain + shift, normal, inverse)


def norm_back(grad_norm, normal, inverse, gain):
    grad_gain = jnp.sum(grad_norm * normal, axis=0)
    grad_shift = jnp.sum(grad_norm, axis=0)
    scaled = grad_norm * gain
    centre_part = jnp.mean(scaled, axis=-1, keepdims=True)
    along_part = normal * jnp.mean(scaled * normal, axis=-1, keepdims=True)
    return (inverse * (scaled - centre_part - along_part), grad_gain, grad_shift)


def matmul(left, right):
    return jnp.dot(left, right, preferred_element_type=jnp.float32)


def dot_first(left, right):
    return lax.dot_general(
        left, right, (((0,), (0,)), ((), ())), preferred_element_type=jnp.float32
    )


def dot_last(left, right):
    return lax.dot_general(
        left, right, (((1,), (1,)), ((), ())), preferred_element_type=jnp.float32
    )


def gelu_tanh(values):
    return jax.nn.gelu(values, approximate=True)


def attend_forward(packed, head_dim):
    length = packed.shape[0]
    local_heads = packed.shape[2] // head_dim
    unpacked = packed.reshape(length, 3, local_heads, head_dim)
    queries = unpacked[:, 0]
    keys_all = unpacked[:, 1]
    values_all = unpacked[:, 2]
    block_rows = min(512, length)
    score_scale = head_dim ** (-0.5)
    key_place = jnp.arange(length)

    def one_block(start):
        query_rows = lax.dynamic_slice_in_dim(queries, start, block_rows, 0)
        scores = (
            jnp.einsum("qhd,khd->hqk", query_rows, keys_all, preferred_element_type=jnp.float32)
            * score_scale
        )
        query_place = start + jnp.arange(block_rows)
        causal = (key_place[None, :] <= query_place[:, None])[None]
        scores = jnp.where(causal, scores, -1e30)
        row_top = jnp.max(scores, axis=-1, keepdims=True)
        exp_scores = jnp.exp(scores - row_top)
        row_total = jnp.sum(exp_scores, axis=-1, keepdims=True)
        probabilities = (exp_scores / row_total).astype(jnp.bfloat16)
        result = jnp.einsum(
            "hqk,khd->qhd", probabilities, values_all, preferred_element_type=jnp.float32
        )
        return (result.astype(jnp.bfloat16), (row_top + jnp.log(row_total))[..., 0])

    block_starts = jnp.arange(length // block_rows) * block_rows
    results, log_totals = lax.map(one_block, block_starts)
    return (results.reshape(length, local_heads * head_dim), log_totals)


def attend_backward(packed, grad_heads, log_totals, head_dim):
    length = packed.shape[0]
    local_heads = packed.shape[2] // head_dim
    unpacked = packed.reshape(length, 3, local_heads, head_dim)
    queries = unpacked[:, 0]
    keys_all = unpacked[:, 1]
    values_all = unpacked[:, 2]
    grad_rows_all = grad_heads.reshape(length, local_heads, head_dim)
    block_rows = min(512, length)
    score_scale = head_dim ** (-0.5)
    key_place = jnp.arange(length)

    def one_block(carry, block_input):
        grad_keys, grad_values = carry
        start, block_lse = block_input
        query_rows = lax.dynamic_slice_in_dim(queries, start, block_rows, 0)
        grad_rows = lax.dynamic_slice_in_dim(grad_rows_all, start, block_rows, 0)
        scores = (
            jnp.einsum("qhd,khd->hqk", query_rows, keys_all, preferred_element_type=jnp.float32)
            * score_scale
        )
        query_place = start + jnp.arange(block_rows)
        causal = (key_place[None, :] <= query_place[:, None])[None]
        scores = jnp.where(causal, scores, -1e30)
        probabilities = jnp.exp(scores - block_lse[..., None])
        grad_probs = jnp.einsum(
            "qhd,khd->hqk", grad_rows, values_all, preferred_element_type=jnp.float32
        )
        grad_values = grad_values + jnp.einsum(
            "hqk,qhd->khd",
            probabilities.astype(jnp.bfloat16),
            grad_rows,
            preferred_element_type=jnp.float32,
        )
        inner = jnp.sum(probabilities * grad_probs, axis=-1, keepdims=True)
        grad_scores = (probabilities * (grad_probs - inner)).astype(jnp.bfloat16)
        grad_query = (
            jnp.einsum("hqk,khd->qhd", grad_scores, keys_all, preferred_element_type=jnp.float32)
            * score_scale
        )
        grad_keys = (
            grad_keys
            + jnp.einsum(
                "hqk,qhd->khd", grad_scores, query_rows, preferred_element_type=jnp.float32
            )
            * score_scale
        )
        return ((grad_keys, grad_values), grad_query)

    empty = jnp.zeros((length, local_heads, head_dim), jnp.float32)
    block_starts = jnp.arange(length // block_rows) * block_rows
    (grad_keys, grad_values), grad_queries = lax.scan(
        one_block, (empty, empty), (block_starts, log_totals)
    )
    grad_queries = grad_queries.reshape(length, local_heads, head_dim)
    stacked = jnp.stack([grad_queries, grad_keys, grad_values], axis=1).astype(jnp.bfloat16)
    return stacked.reshape(length, 3, local_heads * head_dim)


def section_forward(tokens_in, weights):
    gain_rows, shift_rows, bias_row, qkv_matrix, out_matrix, up_matrix, down_matrix = weights
    gain_float = gain_rows.astype(jnp.float32)
    shift_float = shift_rows.astype(jnp.float32)
    row_count = tokens_in.shape[0]
    model_width = out_matrix.shape[0]
    normed = layer_norm(tokens_in, gain_float[0], shift_float[0])[0]
    qkv_bias = jnp.concatenate([shift_float[1], jnp.zeros_like(shift_float[1]), shift_float[2]])
    qkv_tokens = (matmul(normed.astype(jnp.bfloat16), qkv_matrix) + qkv_bias).astype(jnp.bfloat16)
    qkv_heads = lax.all_to_all(
        qkv_tokens.reshape(row_count, 3, model_width),
        "seq",
        split_axis=2,
        concat_axis=0,
        tiled=True,
    )
    attended_heads, log_totals = attend_forward(qkv_heads, HD)
    attended = lax.all_to_all(attended_heads, "seq", split_axis=0, concat_axis=1, tiled=True)
    hidden = tokens_in + matmul(attended, out_matrix) + shift_float[3]
    normed_two = layer_norm(hidden, gain_float[1], shift_float[4])[0]
    upward = matmul(normed_two.astype(jnp.bfloat16), up_matrix) + bias_row.astype(jnp.float32)
    activated = gelu_tanh(upward).astype(jnp.bfloat16)
    result = hidden + matmul(activated, down_matrix) + shift_float[5]
    return (result, (qkv_heads, log_totals, attended, hidden, upward))


def section_backward(grad_out, saved, weights):
    gain_rows, shift_rows, bias_row, qkv_matrix, out_matrix, up_matrix, down_matrix = weights
    gain_float = gain_rows.astype(jnp.float32)
    shift_float = shift_rows.astype(jnp.float32)
    tokens_low, qkv_heads, log_totals, attended, hidden, upward = saved
    tokens_in = tokens_low.astype(jnp.float32)
    row_count = tokens_in.shape[0]
    model_width = out_matrix.shape[0]
    grad_branch = grad_out.astype(jnp.bfloat16)
    activated = gelu_tanh(upward).astype(jnp.bfloat16)
    grad_down = dot_first(activated, grad_branch)
    grad_down_bias = jnp.sum(grad_branch.astype(jnp.float32), axis=0)
    grad_act = dot_last(grad_branch, down_matrix)
    unused, gelu_pull = jax.vjp(gelu_tanh, upward)
    grad_upward = gelu_pull(grad_act)[0].astype(jnp.bfloat16)
    grad_up_bias = jnp.sum(grad_upward.astype(jnp.float32), axis=0)
    normed_two, normal_two, inverse_two = layer_norm(hidden, gain_float[1], shift_float[4])
    grad_up = dot_first(normed_two.astype(jnp.bfloat16), grad_upward)
    grad_normed_two = dot_last(grad_upward, up_matrix)
    grad_from_norm, grad_gain_two, grad_shift_two = norm_back(
        grad_normed_two, normal_two, inverse_two, gain_float[1]
    )
    grad_hidden = grad_out + grad_from_norm
    grad_residual = grad_hidden.astype(jnp.bfloat16)
    grad_out_bias = jnp.sum(grad_residual.astype(jnp.float32), axis=0)
    grad_out_matrix = dot_first(attended, grad_residual)
    grad_attended = dot_last(grad_residual, out_matrix).astype(jnp.bfloat16)
    grad_heads = lax.all_to_all(grad_attended, "seq", split_axis=1, concat_axis=0, tiled=True)
    grad_packed_heads = attend_backward(qkv_heads, grad_heads, log_totals, HD)
    grad_packed = lax.all_to_all(
        grad_packed_heads, "seq", split_axis=0, concat_axis=2, tiled=True
    ).reshape(row_count, 3 * model_width)
    grad_packed_float = grad_packed.astype(jnp.float32)
    grad_query_bias = jnp.sum(grad_packed_float[:, :model_width], axis=0)
    grad_value_bias = jnp.sum(grad_packed_float[:, 2 * model_width :], axis=0)
    normed, normal, inverse = layer_norm(tokens_in, gain_float[0], shift_float[0])
    grad_qkv_matrix = dot_first(normed.astype(jnp.bfloat16), grad_packed)
    grad_normed = dot_last(grad_packed, qkv_matrix)
    grad_from_first, grad_gain_one, grad_shift_one = norm_back(
        grad_normed, normal, inverse, gain_float[0]
    )
    grad_tokens = grad_hidden + grad_from_first
    grad_gains = jnp.stack([grad_gain_one, grad_gain_two])
    grad_shifts = jnp.stack(
        [
            grad_shift_one,
            grad_query_bias,
            grad_value_bias,
            grad_out_bias,
            grad_shift_two,
            grad_down_bias,
        ]
    )
    return (
        grad_tokens,
        (
            grad_gains,
            grad_shifts,
            grad_up_bias,
            grad_qkv_matrix,
            grad_out_matrix,
            grad_up,
            grad_down,
        ),
    )


def swap_cores(block):
    return lax.ppermute(block, "section", [(0, 1), (1, 0)])


def pack_small(gains, shifts, bias):
    pieces = lax.axis_size("dp")
    return jnp.concatenate(
        [
            jnp.moveaxis(gains.reshape(gains.shape[0], pieces, -1), 1, 0).reshape(pieces, -1),
            jnp.moveaxis(shifts.reshape(shifts.shape[0], pieces, -1), 1, 0).reshape(pieces, -1),
            bias.reshape(pieces, -1),
        ],
        axis=1,
    )


def half_sum(grad, is_first, after=None):
    half = grad.shape[1] // 2
    low, high = grad[:, :half], grad[:, half:]
    away = jnp.where(is_first, high, low).astype(jnp.bfloat16)
    total = jnp.where(is_first, low, high) + swap_cores(away).astype(jnp.float32)
    own_rows = lax.psum_scatter(total.astype(jnp.bfloat16), "dp", scatter_dimension=0, tiled=True)
    if after is not None:
        own_rows = lax.optimization_barrier((own_rows, after))[0]
    return lax.psum(own_rows, "seq")


def shards(
    section_ends,
    live,
    norm_gains,
    offsets,
    expand_bias,
    query_key_value,
    attention_out,
    expand_weight,
    contract_weight,
):
    core = lax.axis_index("section")
    is_first = core == 0
    local_ends = section_ends[0, :, 0]
    live_float = live[:, 0].astype(jnp.float32)
    gain_size, shift_size, bias_size = norm_gains[0].size, offsets[0].size, expand_bias[0].size
    width = norm_gains.shape[2]

    kept = jnp.where(is_first, local_ends[0], local_ends[1])
    came = swap_cores(jnp.where(is_first, local_ends[1], local_ends[0]))
    tokens_first = jnp.where(is_first, kept, came)
    own_live = jnp.where(is_first, live_float[0], live_float[1])
    cotangent = jnp.where(is_first, came, kept).astype(jnp.float32) * own_live

    small = jnp.concatenate(
        [norm_gains[0].reshape(-1), offsets[0].reshape(-1), expand_bias[0].reshape(-1)]
    )
    small = lax.all_gather(small[None], "dp", axis=0, tiled=True)
    pieces = small.shape[0]
    gathered = [small] + [
        lax.all_gather(a[0], "dp", axis=0, tiled=True)
        for a in (query_key_value, attention_out, expand_weight, contract_weight)
    ]
    others = [swap_cores(a) for a in gathered]

    def layer_weights(chosen):
        low = chosen[0]
        gains = jnp.moveaxis(low[:, :gain_size].reshape(pieces, 2, width), 0, 1).reshape(2, -1)
        shifts = jnp.moveaxis(
            low[:, gain_size : gain_size + shift_size].reshape(pieces, 6, width), 0, 1
        ).reshape(6, -1)
        bias = low[:, gain_size + shift_size :].reshape(-1)
        return (gains, shifts, bias) + tuple(chosen[1:])

    weights_zero = layer_weights([jnp.where(is_first, a, b) for a, b in zip(gathered, others)])
    weights_one = layer_weights([jnp.where(is_first, b, a) for a, b in zip(gathered, others)])

    middle, saved_zero = section_forward(tokens_first.astype(jnp.float32), weights_zero)
    tokens_second = middle.astype(jnp.bfloat16)
    result, saved_one = section_forward(tokens_second.astype(jnp.float32), weights_one)
    grad_middle, grads_one = section_backward(
        cotangent, (tokens_second,) + saved_one, weights_one
    )
    halves_one = [half_sum(g, is_first) for g in grads_one[3:]]
    grad_middle = grad_middle.astype(jnp.bfloat16).astype(jnp.float32)
    grad_first, grads_zero = section_backward(
        grad_middle, (tokens_first,) + saved_zero, weights_zero
    )
    halves_zero = [half_sum(g, is_first, halves_one) for g in grads_zero[3:]]

    small_zero, small_one = pack_small(*grads_zero[:3]), pack_small(*grads_one[:3])
    small_sum = jnp.where(is_first, small_zero, small_one) + swap_cores(
        jnp.where(is_first, small_one, small_zero)
    )
    small_sum = lax.psum(
        lax.psum_scatter(small_sum, "dp", scatter_dimension=0, tiled=True), "seq"
    )[0]
    final_small = (
        small_sum[:gain_size].reshape(1, 2, width),
        small_sum[gain_size : gain_size + shift_size].reshape(1, 6, width),
        small_sum[gain_size + shift_size :].reshape(1, bias_size),
    )

    final_large = []
    for zero, one in zip(halves_zero, halves_one):
        mine = jnp.where(is_first, zero, one)
        arrived = swap_cores(jnp.where(is_first, one, zero))
        left = jnp.where(is_first, mine, arrived)
        right = jnp.where(is_first, arrived, mine)
        final_large.append(jnp.concatenate([left, right], axis=1).astype(jnp.float32)[None])

    result = result * own_live
    stays = jnp.where(is_first, grad_first, result)
    comes = swap_cores(jnp.where(is_first, result, grad_first))
    edges = jnp.stack([jnp.where(is_first, stays, comes), jnp.where(is_first, comes, stays)])
    return (edges[None, :, None],) + final_small + tuple(final_large)


def solution(mesh):
    return jax.shard_map(
        shards,
        mesh=mesh,
        in_specs=(
            P("section", None, "dp", "seq", None),
            P(None, "dp"),
            P("section", None, "dp"),
            P("section", None, "dp"),
            P("section", "dp"),
            P("section", "dp", None),
            P("section", "dp", None),
            P("section", "dp", None),
            P("section", "dp", None),
        ),
        out_specs=(
            P("section", None, "dp", "seq", None),
            P("section", None, "dp"),
            P("section", None, "dp"),
            P("section", "dp"),
            P("section", "dp", None),
            P("section", "dp", None),
            P("section", "dp", None),
            P("section", "dp", None),
        ),
        check_vma=False,
    )
```

```python
import jax
import jax.numpy as jnp
from jax import lax
from jax.sharding import PartitionSpec as P

HD = 64


EPSILON = 1e-05


def layer_norm(values, gain, shift):
    row_mean = jnp.mean(values, axis=-1, keepdims=True)
    centred = values - row_mean
    variance = jnp.mean(centred * centred, axis=-1, keepdims=True)
    inverse = lax.rsqrt(variance + EPSILON)
    normal = centred * inverse
    return (normal * gain + shift, normal, inverse)


def norm_back(grad_norm, normal, inverse, gain):
    grad_gain = jnp.sum(grad_norm * normal, axis=0)
    grad_shift = jnp.sum(grad_norm, axis=0)
    scaled = grad_norm * gain
    centre_part = jnp.mean(scaled, axis=-1, keepdims=True)
    along_part = normal * jnp.mean(scaled * normal, axis=-1, keepdims=True)
    return (inverse * (scaled - centre_part - along_part), grad_gain, grad_shift)


def matmul(left, right):
    return jnp.dot(left, right, preferred_element_type=jnp.float32)


def dot_first(left, right):
    return lax.dot_general(
        left, right, (((0,), (0,)), ((), ())), preferred_element_type=jnp.float32
    )


def dot_last(left, right):
    return lax.dot_general(
        left, right, (((1,), (1,)), ((), ())), preferred_element_type=jnp.float32
    )


def gelu_tanh(values):
    return jax.nn.gelu(values, approximate=True)


def attend_forward(packed, head_dim):
    length = packed.shape[0]
    local_heads = packed.shape[2] // head_dim
    unpacked = packed.reshape(length, 3, local_heads, head_dim)
    queries = unpacked[:, 0]
    keys_all = unpacked[:, 1]
    values_all = unpacked[:, 2]
    block_rows = min(512, length)
    score_scale = head_dim ** (-0.5)
    key_place = jnp.arange(length)

    def one_block(start):
        query_rows = lax.dynamic_slice_in_dim(queries, start, block_rows, 0)
        scores = (
            jnp.einsum("qhd,khd->hqk", query_rows, keys_all, preferred_element_type=jnp.float32)
            * score_scale
        )
        query_place = start + jnp.arange(block_rows)
        causal = (key_place[None, :] <= query_place[:, None])[None]
        scores = jnp.where(causal, scores, -1e30)
        row_top = jnp.max(scores, axis=-1, keepdims=True)
        exp_scores = jnp.exp(scores - row_top)
        row_total = jnp.sum(exp_scores, axis=-1, keepdims=True)
        probabilities = (exp_scores / row_total).astype(jnp.bfloat16)
        result = jnp.einsum(
            "hqk,khd->qhd", probabilities, values_all, preferred_element_type=jnp.float32
        )
        return (result.astype(jnp.bfloat16), (row_top + jnp.log(row_total))[..., 0])

    block_starts = jnp.arange(length // block_rows) * block_rows
    results, log_totals = lax.map(one_block, block_starts)
    return (results.reshape(length, local_heads * head_dim), log_totals)


def attend_backward(packed, grad_heads, log_totals, head_dim):
    length = packed.shape[0]
    local_heads = packed.shape[2] // head_dim
    unpacked = packed.reshape(length, 3, local_heads, head_dim)
    queries = unpacked[:, 0]
    keys_all = unpacked[:, 1]
    values_all = unpacked[:, 2]
    grad_rows_all = grad_heads.reshape(length, local_heads, head_dim)
    block_rows = min(512, length)
    score_scale = head_dim ** (-0.5)
    key_place = jnp.arange(length)

    def one_block(carry, block_input):
        grad_keys, grad_values = carry
        start, block_lse = block_input
        query_rows = lax.dynamic_slice_in_dim(queries, start, block_rows, 0)
        grad_rows = lax.dynamic_slice_in_dim(grad_rows_all, start, block_rows, 0)
        scores = (
            jnp.einsum("qhd,khd->hqk", query_rows, keys_all, preferred_element_type=jnp.float32)
            * score_scale
        )
        query_place = start + jnp.arange(block_rows)
        causal = (key_place[None, :] <= query_place[:, None])[None]
        scores = jnp.where(causal, scores, -1e30)
        probabilities = jnp.exp(scores - block_lse[..., None])
        grad_probs = jnp.einsum(
            "qhd,khd->hqk", grad_rows, values_all, preferred_element_type=jnp.float32
        )
        grad_values = grad_values + jnp.einsum(
            "hqk,qhd->khd",
            probabilities.astype(jnp.bfloat16),
            grad_rows,
            preferred_element_type=jnp.float32,
        )
        inner = jnp.sum(probabilities * grad_probs, axis=-1, keepdims=True)
        grad_scores = (probabilities * (grad_probs - inner)).astype(jnp.bfloat16)
        grad_query = (
            jnp.einsum("hqk,khd->qhd", grad_scores, keys_all, preferred_element_type=jnp.float32)
            * score_scale
        )
        grad_keys = (
            grad_keys
            + jnp.einsum(
                "hqk,qhd->khd", grad_scores, query_rows, preferred_element_type=jnp.float32
            )
            * score_scale
        )
        return ((grad_keys, grad_values), grad_query)

    empty = jnp.zeros((length, local_heads, head_dim), jnp.float32)
    block_starts = jnp.arange(length // block_rows) * block_rows
    (grad_keys, grad_values), grad_queries = lax.scan(
        one_block, (empty, empty), (block_starts, log_totals)
    )
    grad_queries = grad_queries.reshape(length, local_heads, head_dim)
    stacked = jnp.stack([grad_queries, grad_keys, grad_values], axis=1).astype(jnp.bfloat16)
    return stacked.reshape(length, 3, local_heads * head_dim)


def section_forward(tokens_in, weights):
    gain_rows, shift_rows, bias_row, qkv_matrix, out_matrix, up_matrix, down_matrix = weights
    gain_float = gain_rows.astype(jnp.float32)
    shift_float = shift_rows.astype(jnp.float32)
    row_count = tokens_in.shape[0]
    model_width = out_matrix.shape[0]
    normed = layer_norm(tokens_in, gain_float[0], shift_float[0])[0]
    qkv_bias = jnp.concatenate([shift_float[1], jnp.zeros_like(shift_float[1]), shift_float[2]])
    qkv_tokens = (matmul(normed.astype(jnp.bfloat16), qkv_matrix) + qkv_bias).astype(jnp.bfloat16)
    qkv_heads = lax.all_to_all(
        qkv_tokens.reshape(row_count, 3, model_width),
        "seq",
        split_axis=2,
        concat_axis=0,
        tiled=True,
    )
    attended_heads, log_totals = attend_forward(qkv_heads, HD)
    attended = lax.all_to_all(attended_heads, "seq", split_axis=0, concat_axis=1, tiled=True)
    hidden = tokens_in + matmul(attended, out_matrix) + shift_float[3]
    normed_two = layer_norm(hidden, gain_float[1], shift_float[4])[0]
    upward = matmul(normed_two.astype(jnp.bfloat16), up_matrix) + bias_row.astype(jnp.float32)
    activated = gelu_tanh(upward).astype(jnp.bfloat16)
    result = hidden + matmul(activated, down_matrix) + shift_float[5]
    return (result, (qkv_heads, log_totals, attended, hidden, upward))


def section_backward(grad_out, saved, weights):
    gain_rows, shift_rows, bias_row, qkv_matrix, out_matrix, up_matrix, down_matrix = weights
    gain_float = gain_rows.astype(jnp.float32)
    shift_float = shift_rows.astype(jnp.float32)
    tokens_low, qkv_heads, log_totals, attended, hidden, upward = saved
    tokens_in = tokens_low.astype(jnp.float32)
    row_count = tokens_in.shape[0]
    model_width = out_matrix.shape[0]
    grad_branch = grad_out.astype(jnp.bfloat16)
    activated = gelu_tanh(upward).astype(jnp.bfloat16)
    grad_down = dot_first(activated, grad_branch)
    grad_down_bias = jnp.sum(grad_branch.astype(jnp.float32), axis=0)
    grad_act = dot_last(grad_branch, down_matrix)
    unused, gelu_pull = jax.vjp(gelu_tanh, upward)
    grad_upward = gelu_pull(grad_act)[0].astype(jnp.bfloat16)
    grad_up_bias = jnp.sum(grad_upward.astype(jnp.float32), axis=0)
    normed_two, normal_two, inverse_two = layer_norm(hidden, gain_float[1], shift_float[4])
    grad_up = dot_first(normed_two.astype(jnp.bfloat16), grad_upward)
    grad_normed_two = dot_last(grad_upward, up_matrix)
    grad_from_norm, grad_gain_two, grad_shift_two = norm_back(
        grad_normed_two, normal_two, inverse_two, gain_float[1]
    )
    grad_hidden = grad_out + grad_from_norm
    grad_residual = grad_hidden.astype(jnp.bfloat16)
    grad_out_bias = jnp.sum(grad_residual.astype(jnp.float32), axis=0)
    grad_out_matrix = dot_first(attended, grad_residual)
    grad_attended = dot_last(grad_residual, out_matrix).astype(jnp.bfloat16)
    grad_heads = lax.all_to_all(grad_attended, "seq", split_axis=1, concat_axis=0, tiled=True)
    grad_packed_heads = attend_backward(qkv_heads, grad_heads, log_totals, HD)
    grad_packed = lax.all_to_all(
        grad_packed_heads, "seq", split_axis=0, concat_axis=2, tiled=True
    ).reshape(row_count, 3 * model_width)
    grad_packed_float = grad_packed.astype(jnp.float32)
    grad_query_bias = jnp.sum(grad_packed_float[:, :model_width], axis=0)
    grad_value_bias = jnp.sum(grad_packed_float[:, 2 * model_width :], axis=0)
    normed, normal, inverse = layer_norm(tokens_in, gain_float[0], shift_float[0])
    grad_qkv_matrix = dot_first(normed.astype(jnp.bfloat16), grad_packed)
    grad_normed = dot_last(grad_packed, qkv_matrix)
    grad_from_first, grad_gain_one, grad_shift_one = norm_back(
        grad_normed, normal, inverse, gain_float[0]
    )
    grad_tokens = grad_hidden + grad_from_first
    grad_gains = jnp.stack([grad_gain_one, grad_gain_two])
    grad_shifts = jnp.stack(
        [
            grad_shift_one,
            grad_query_bias,
            grad_value_bias,
            grad_out_bias,
            grad_shift_two,
            grad_down_bias,
        ]
    )
    return (
        grad_tokens,
        (
            grad_gains,
            grad_shifts,
            grad_up_bias,
            grad_qkv_matrix,
            grad_out_matrix,
            grad_up,
            grad_down,
        ),
    )


def swap_cores(block):
    return lax.ppermute(block, "section", [(0, 1), (1, 0)])


def pack_small(gains, shifts, bias):
    pieces = lax.axis_size("dp")
    return jnp.concatenate(
        [
            jnp.moveaxis(gains.reshape(gains.shape[0], pieces, -1), 1, 0).reshape(pieces, -1),
            jnp.moveaxis(shifts.reshape(shifts.shape[0], pieces, -1), 1, 0).reshape(pieces, -1),
            bias.reshape(pieces, -1),
        ],
        axis=1,
    )


def half_sum(grad, is_first, after=None):
    half = grad.shape[1] // 2
    low, high = grad[:, :half], grad[:, half:]
    away = jnp.where(is_first, high, low).astype(jnp.bfloat16)
    total = jnp.where(is_first, low, high) + swap_cores(away).astype(jnp.float32)
    own_rows = lax.psum_scatter(total.astype(jnp.bfloat16), "dp", scatter_dimension=0, tiled=True)
    if after is not None:
        own_rows = lax.optimization_barrier((own_rows, after))[0]
    return lax.psum(own_rows, "seq")


def shards(
    section_ends,
    live,
    norm_gains,
    offsets,
    expand_bias,
    query_key_value,
    attention_out,
    expand_weight,
    contract_weight,
):
    core = lax.axis_index("section")
    is_first = core == 0
    local_ends = section_ends[0, :, 0]
    live_float = live[:, 0].astype(jnp.float32)
    gain_size, shift_size, bias_size = norm_gains[0].size, offsets[0].size, expand_bias[0].size
    width = norm_gains.shape[2]

    kept = jnp.where(is_first, local_ends[0], local_ends[1])
    came = swap_cores(jnp.where(is_first, local_ends[1], local_ends[0]))
    tokens_first = jnp.where(is_first, kept, came)
    own_live = jnp.where(is_first, live_float[0], live_float[1])
    cotangent = jnp.where(is_first, came, kept).astype(jnp.float32) * own_live

    small = jnp.concatenate(
        [norm_gains[0].reshape(-1), offsets[0].reshape(-1), expand_bias[0].reshape(-1)]
    )
    small = lax.all_gather(small[None], "dp", axis=0, tiled=True)
    pieces = small.shape[0]
    gathered = [small] + [
        lax.all_gather(a[0], "dp", axis=0, tiled=True)
        for a in (query_key_value, attention_out, expand_weight, contract_weight)
    ]
    others = [swap_cores(a) for a in gathered]

    def layer_weights(chosen):
        low = chosen[0]
        gains = jnp.moveaxis(low[:, :gain_size].reshape(pieces, 2, width), 0, 1).reshape(2, -1)
        shifts = jnp.moveaxis(
            low[:, gain_size : gain_size + shift_size].reshape(pieces, 6, width), 0, 1
        ).reshape(6, -1)
        bias = low[:, gain_size + shift_size :].reshape(-1)
        return (gains, shifts, bias) + tuple(chosen[1:])

    weights_zero = layer_weights([jnp.where(is_first, a, b) for a, b in zip(gathered, others)])
    weights_one = layer_weights([jnp.where(is_first, b, a) for a, b in zip(gathered, others)])

    middle, saved_zero = section_forward(tokens_first.astype(jnp.float32), weights_zero)
    tokens_second = middle.astype(jnp.bfloat16)
    result, saved_one = section_forward(tokens_second.astype(jnp.float32), weights_one)
    grad_middle, grads_one = section_backward(
        cotangent, (tokens_second,) + saved_one, weights_one
    )
    halves_one = [half_sum(g, is_first) for g in grads_one[3:]]
    grad_middle = grad_middle.astype(jnp.bfloat16).astype(jnp.float32)
    grad_first, grads_zero = section_backward(
        grad_middle, (tokens_first,) + saved_zero, weights_zero
    )
    halves_zero = [half_sum(g, is_first, halves_one) for g in grads_zero[3:]]

    small_zero, small_one = pack_small(*grads_zero[:3]), pack_small(*grads_one[:3])
    small_sum = jnp.where(is_first, small_zero, small_one) + swap_cores(
        jnp.where(is_first, small_one, small_zero)
    )
    small_sum = lax.psum(small_sum, ("dp", "seq"))
    small_sum = lax.dynamic_index_in_dim(small_sum, lax.axis_index("dp"), 0, keepdims=False)
    final_small = (
        small_sum[:gain_size].reshape(1, 2, width),
        small_sum[gain_size : gain_size + shift_size].reshape(1, 6, width),
        small_sum[gain_size + shift_size :].reshape(1, bias_size),
    )

    final_large = []
    for zero, one in zip(halves_zero, halves_one):
        mine = jnp.where(is_first, zero, one)
        arrived = swap_cores(jnp.where(is_first, one, zero))
        left = jnp.where(is_first, mine, arrived)
        right = jnp.where(is_first, arrived, mine)
        final_large.append(jnp.concatenate([left, right], axis=1).astype(jnp.float32)[None])

    result = result * own_live
    stays = jnp.where(is_first, grad_first, result)
    comes = swap_cores(jnp.where(is_first, result, grad_first))
    edges = jnp.stack([jnp.where(is_first, stays, comes), jnp.where(is_first, comes, stays)])
    return (edges[None, :, None],) + final_small + tuple(final_large)


def solution(mesh):
    return jax.shard_map(
        shards,
        mesh=mesh,
        in_specs=(
            P("section", None, "dp", "seq", None),
            P(None, "dp"),
            P("section", None, "dp"),
            P("section", None, "dp"),
            P("section", "dp"),
            P("section", "dp", None),
            P("section", "dp", None),
            P("section", "dp", None),
            P("section", "dp", None),
        ),
        out_specs=(
            P("section", None, "dp", "seq", None),
            P("section", None, "dp"),
            P("section", None, "dp"),
            P("section", "dp"),
            P("section", "dp", None),
            P("section", "dp", None),
            P("section", "dp", None),
            P("section", "dp", None),
        ),
        check_vma=False,
    )
```
